32 devices in a mesh: date: 2 (over core), space: 16 (over z, y, x).
Axes of the slice: x: 2, y: 2, z: 4, core: 2. Of those that a mesh axis runs over, the one named last changes fastest.
Arguments:
- acquisitions: bfloat16 [16, 2048, 512], P('date', 'space')
- partner: int32 [16, 9], replicated, may hold values from 0 to 15, as said below
- pair_count: int32 [16], replicated, may hold values from 2 to 9, as said below
- band_low: int32 [16, 9], P('date'), may hold values from 0 to 95
- band_high: int32 [16, 9], P('date'), may hold values from 160 to 256
Outputs:
- coherence: bfloat16 [16, 9, 2048, 512], P('date', None, 'space')
The draws below stay inside these ranges and needn't reach their ends.
Inputs may be any that keep to these rules, and one draw needn't show every extreme that they name: For j < pair_count[d], partner[d, j] is the secondary date of pair j of date d; other slots name any date but no pair. A secondary never lies in its reference's block of 8 dates (one index of date), and the pairs of one block name at most 4 distinct dates of any other block; some two blocks reach 4. The pairs of date d are its first pair_count[d] slots.
All inputs are finite; a program needn't handle non-finite values.
Results may differ from the reference program's by a relative error of at most 0.0085.
Values may be sent and summed in bfloat16 or wider, within the bound.
No kernel may reach another device: no remote copies, remote signals or barrier semaphores. Data moves between devices by JAX's collectives and lax.ppermute only.
A program may use at most 192 MiB of HBM per device.

```python
import math
import jax
import jax.numpy as jnp
from jax import lax

RANGE = 256
MAXP = 9
DATES_DEV = 8
DATES = 16
ROWS = 2048


def draw_acquisitions(key, part):
    subkeys = jax.random.split(key, 5)
    shape = (DATES, ROWS, 2 * RANGE)
    common = jax.random.truncated_normal(subkeys[0], -6.0, 6.0, (ROWS, 2 * RANGE), jnp.float32)
    noise_part = jax.random.truncated_normal(subkeys[1], -6.0, 6.0, shape, jnp.float32)
    weight = jax.random.uniform(subkeys[2], (DATES, 1, 1), jnp.float32, 0.3, 0.9)
    scale_low = 0.15
    scale_high = 1.5
    row_scale = jnp.exp(jax.random.uniform(subkeys[3], (DATES, ROWS, 1), jnp.float32, math.log(scale_low), math.log(scale_high)))
    col_part = jnp.exp(jax.random.uniform(subkeys[4], (1, 1, RANGE), jnp.float32, math.log(scale_low), math.log(scale_high)))
    col_scale = jnp.concatenate([col_part, col_part], axis=2)
    mixed_part = weight * common[None] + jnp.sqrt(1.0 - weight * weight) * noise_part
    return (row_scale * col_scale * mixed_part).astype(jnp.bfloat16)


def draw_pair_count(key, part):
    subkeys = jax.random.split(key, 5)
    groups = DATES // DATES_DEV
    busy_group = jax.random.randint(subkeys[0], (groups,), 0, 4) == 0
    forced = jax.random.randint(subkeys[1], (), 0, groups)
    group_ids = jnp.arange(groups, dtype=jnp.int32)
    busy_group = busy_group | (group_ids == forced)
    busy_dates = jnp.repeat(busy_group, DATES_DEV)
    busy_count = jax.random.randint(subkeys[2], (DATES,), 7, MAXP + 1)
    quiet_count = jax.random.randint(subkeys[3], (DATES,), 2, 5)
    counts = jnp.where(busy_dates, busy_count, quiet_count)
    date_ids = jnp.arange(DATES, dtype=jnp.int32)
    counts = jnp.where(date_ids // DATES_DEV == forced, MAXP, counts)
    drawn_date = (forced + 1) % groups * DATES_DEV + jax.random.randint(subkeys[4], (), 0, DATES_DEV)
    counts = jnp.where(date_ids == drawn_date, 2, counts)
    return counts.astype(jnp.int32)


def draw_partner(key, part):
    subkeys = jax.random.split(key, 3)
    groups = DATES // DATES_DEV
    capacity = DATES_DEV // 2
    date_ids = jnp.arange(DATES, dtype=jnp.int32)
    home_block = date_ids // DATES_DEV
    local_index = date_ids % DATES_DEV
    slot_ids = jnp.arange(MAXP, dtype=jnp.int32)
    reach = jax.random.randint(subkeys[0], (groups, MAXP), 1, groups // 2 + 1)
    forward_pick = jax.random.randint(subkeys[1], (groups, MAXP), 0, 2) == 1
    offset_table = jax.random.randint(subkeys[2], (groups, groups), 0, DATES_DEV)
    device_step = reach[home_block]
    forward_ok = home_block[:, None] + device_step < groups
    backward_ok = home_block[:, None] - device_step >= 0
    target_block = jnp.where(forward_pick[home_block] & forward_ok | jnp.logical_not(backward_ok), home_block[:, None] + device_step, home_block[:, None] - device_step)
    block_offset = offset_table[home_block[:, None], target_block]
    within_block = (block_offset + (local_index[:, None] + slot_ids[None, :]) % capacity) % DATES_DEV
    live_partner = (target_block * DATES_DEV + within_block).astype(jnp.int32)
    counts = draw_pair_count(key, part)
    dead_partner = jax.random.randint(jax.random.fold_in(key, 7919), (DATES, MAXP), 0, DATES)
    is_live = slot_ids[None, :] < counts[:, None]
    return jnp.where(is_live, live_partner, dead_partner).astype(jnp.int32)


def touch_ends(values, rng, smallest, largest):
    longest = values.shape.index(max(values.shape))
    spots = []
    for shift in (0, 1):
        where = [jax.random.randint(jax.random.fold_in(rng, axis), (), 0, length) for axis, length in enumerate(values.shape)]
        where[longest] = (where[longest] + shift) % values.shape[longest]
        spots.append(tuple(where))
    return values.at[spots[0]].set(smallest).at[spots[1]].set(largest)


def setup_inputs(seed: int = 0) -> dict:
    key_of = jax.random.split(jax.random.key(seed), 6)
    acquisitions = draw_acquisitions(jax.random.fold_in(key_of[5], 71), 0)
    partner = draw_partner(jax.random.fold_in(key_of[5], 71), 0)
    pair_count = draw_pair_count(jax.random.fold_in(key_of[5], 71), 0)
    band_low = touch_ends(jax.random.randint(key_of[3], (DATES, MAXP), 0, RANGE * 3 // 8), jax.random.fold_in(key_of[3], 1), 0, (RANGE * 3 // 8) - 1).astype(jnp.int32)
    band_high = touch_ends(jax.random.randint(key_of[4], (DATES, MAXP), RANGE * 5 // 8, RANGE + 1), jax.random.fold_in(key_of[4], 1), RANGE * 5 // 8, RANGE).astype(jnp.int32)
    return {"acquisitions": acquisitions, "partner": partner, "pair_count": pair_count, "band_low": band_low, "band_high": band_high}


def tables(range_bins):
    bin_ids = jnp.arange(range_bins, dtype=jnp.int32)
    phase_index = bin_ids[:, None] * bin_ids[None, :] % range_bins
    angles = phase_index.astype(jnp.float32) * (2.0 * math.pi / range_bins)
    cosine = jnp.cos(angles)
    sine_part = jnp.sin(angles)
    forward = jnp.concatenate([jnp.concatenate([cosine, -sine_part], 1), jnp.concatenate([sine_part, cosine], 1)], 0)
    inverse = jnp.concatenate([jnp.concatenate([cosine, sine_part], 1), jnp.concatenate([-sine_part, cosine], 1)], 0)
    return (forward.astype(jnp.bfloat16), inverse.astype(jnp.bfloat16))

def window_sums(stacked_field, range_bins):
    widened = jnp.pad(stacked_field, [(0, 0)] * (stacked_field.ndim - 1) + [(4, 4)])
    across = widened[..., 0:range_bins]
    for offset_col in range(1, 9):
        across = across + widened[..., offset_col:offset_col + range_bins]
    return across[..., :-2, :] + across[..., 1:-1, :] + across[..., 2:, :]

def reference(acquisitions, partner, pair_count, band_low, band_high):
    forward, inverse = tables(RANGE)
    range_cols = 2 * RANGE
    spectra = jnp.dot(acquisitions.reshape(-1, range_cols), forward, preferred_element_type=jnp.float32)
    spectra = spectra.astype(jnp.bfloat16).reshape(DATES, ROWS, range_cols)
    bin_index = jnp.arange(range_cols, dtype=jnp.int32) % RANGE
    inverse_size = 1.0 / RANGE

    def one_pair(pair_index):
        date_id = pair_index // MAXP
        slot_id = pair_index % MAXP
        is_live = slot_id < pair_count[date_id]

        def compute_pair():
            second = partner[date_id, slot_id]
            low_bin = band_low[date_id, slot_id]
            high_bin = band_high[date_id, slot_id]
            band_mask = ((bin_index >= low_bin) & (bin_index < high_bin)).astype(jnp.bfloat16)
            ref_spec = lax.dynamic_index_in_dim(spectra, date_id, 0, keepdims=False) * band_mask
            sec_spec = lax.dynamic_index_in_dim(spectra, second, 0, keepdims=False) * band_mask
            filt_ref = jnp.dot(ref_spec, inverse, preferred_element_type=jnp.float32) * inverse_size
            filt_sec = jnp.dot(sec_spec, inverse, preferred_element_type=jnp.float32) * inverse_size
            ref_re, ref_im = (filt_ref[:, :RANGE], filt_ref[:, RANGE:])
            sec_re, sec_im = (filt_sec[:, :RANGE], filt_sec[:, RANGE:])
            fields = jnp.stack([ref_re * sec_re + ref_im * sec_im, ref_im * sec_re - ref_re * sec_im, ref_re * ref_re + ref_im * ref_im, sec_re * sec_re + sec_im * sec_im])
            framed = jnp.pad(fields, ((0, 0), (1, 1), (0, 0)))
            looked = window_sums(framed, RANGE)
            normalizer = 1.0 / jnp.sqrt(jnp.maximum(looked[2], 1.0) * jnp.maximum(looked[3], 1.0))
            return jnp.concatenate([looked[0] * normalizer, looked[1] * normalizer], -1).astype(jnp.bfloat16)

        def empty_out():
            return jnp.zeros((ROWS, range_cols), jnp.bfloat16)
        return lax.cond(is_live, compute_pair, empty_out)
    result = lax.map(one_pair, jnp.arange(DATES * MAXP, dtype=jnp.int32))
    return result.reshape(DATES, MAXP, ROWS, range_cols)
```

```python
import functools

import jax
import jax.numpy as jnp
import ml_dtypes
import numpy as np
from jax import lax
from jax.experimental import pallas as pl
from jax.experimental.pallas import tpu as pltpu
from jax.sharding import PartitionSpec as P

BF = jnp.bfloat16
F32 = jnp.float32
LANES = 16
GROUP = 3


def constants(bins, rows):
    k = np.arange(bins)
    angle = (k[:, None] * k[None, :] % bins) * (2.0 * np.pi / bins)
    cosine, sine = np.cos(angle), np.sin(angle)
    forward = np.block([[cosine, -sine], [sine, cosine]])
    inverse = np.block([[cosine, sine], [-sine, cosine]]) / bins
    half = bins // 2
    even, odd = np.arange(0, bins, 2), np.arange(1, bins, 2)
    even, odd = np.concatenate([even, bins + even]), np.concatenate([odd, bins + odd])
    first = np.concatenate([np.arange(half), bins + np.arange(half)])
    band = np.abs(k[:, None] - k[None, :]) <= 4
    tiles = rows // LANES
    order = np.zeros(((tiles + 2) * LANES, rows))
    for g in range(-1, tiles + 1):
        for s in range(LANES):
            row = s * tiles + g
            if 0 <= row < rows:
                order[(g + 1) * LANES + s, row] = 1
    made = (forward[:, np.concatenate([even, odd])], inverse[even][:, first], inverse[odd][:, first], band, order)
    return [jnp.asarray(m.astype(np.float32).astype(ml_dtypes.bfloat16)) for m in made]


def dot(a, b):
    return lax.dot_general(a, b, (((1,), (0,)), ((), ())), preferred_element_type=F32)


def pairs_kernel(
    block, count, partner, low, high, *refs, blocks
):
    strips, refs = refs[:blocks], refs[blocks:]
    edges, refs = refs[:blocks], refs[blocks:]
    forward, inv_even, inv_odd, band, order, out, spectra, turned = refs
    date = pl.program_id(0)
    dates, rows, cols = strips[0].shape
    slots = out.shape[1]
    ext = spectra.shape[1]
    bins = cols // 2
    half = bins // 2

    @pl.when(date == 0)
    def _():
        table, place = forward[...], order[...]
        row_id = lax.broadcasted_iota(jnp.int32, (ext, 2 * dates), 0)
        col_id = lax.broadcasted_iota(jnp.int32, (ext, 2 * dates), 1)
        for k in range(blocks):
            edge = dot(edges[k][...], table).astype(BF)
            for q in range(dates):
                at_edge = ((row_id == 0) & (col_id == q)) | ((row_id == ext - 1) & (col_id == dates + q))
                spectrum = dot(strips[k][q], table).astype(BF)
                put = jnp.where(at_edge, 1.0, 0.0).astype(BF)
                spectra[k * dates + q] = (dot(place, spectrum) + dot(put, edge)).astype(BF)

    lane = lax.broadcasted_iota(jnp.int32, (LANES, cols), 1)
    bin_id = lane % half * 2 + lane // bins
    here = block[0]
    whole_date = here * dates + date
    even, odd, window = inv_even[...], inv_odd[...], band[...]

    def masked(slot):
        live = slot < count[whole_date]
        low_bin = jnp.where(live, low[date, slot], 0)
        high_bin = jnp.where(live, high[date, slot], 0)
        mask = jnp.where((bin_id >= low_bin) & (bin_id < high_bin), 1.0, 0.0).astype(BF)[None]
        second = partner[whole_date, slot]
        away = second // dates - here
        away = jnp.where(away < 0, away + blocks, away)
        tiled = (ext // LANES, LANES, cols)
        a = (spectra[date].reshape(tiled) * mask).reshape(ext, cols)
        b = (spectra[away * dates + second % dates].reshape(tiled) * mask).reshape(ext, cols)
        return [a, b]

    def some_slots(step, _):
        group = [step * GROUP + i for i in range(GROUP)]
        x = jnp.concatenate([m for slot in group for m in masked(slot)], 0)
        e = dot(x[:, :bins], even)
        o = dot(x[:, bins:], odd)
        halves = ((e + o).astype(BF), (e - o).astype(BF))
        sums = []
        for i in range(GROUP):
            fields = []
            for v in halves:
                a, b = v[2 * i * ext : (2 * i + 1) * ext], v[(2 * i + 1) * ext : (2 * i + 2) * ext]
                a_re, a_im, b_re, b_im = a[:, :half], a[:, half:], b[:, :half], b[:, half:]
                fields.append(
                    [
                        a_re * b_re + a_im * b_im,
                        a_im * b_re - a_re * b_im,
                        a_re * a_re + a_im * a_im,
                        b_re * b_re + b_im * b_im,
                    ]
                )
            for first, second in zip(*fields):
                f = jnp.concatenate([first, second], 1)
                sums.append(f[:rows] + f[LANES : LANES + rows] + f[2 * LANES :])
        looked = dot(jnp.concatenate(sums, 0), window)
        for i, slot in enumerate(group):
            cross_re, cross_im, power_ref, power_sec = [
                looked[(4 * i + q) * rows : (4 * i + q + 1) * rows] for q in range(4)
            ]
            scale = lax.rsqrt(jnp.maximum(power_ref, 1.0) * jnp.maximum(power_sec, 1.0))
            re, im = cross_re * scale, cross_im * scale
            tiles = rows // LANES
            for c, v in enumerate((re[:, :half], re[:, half:], im[:, :half], im[:, half:])):
                for g in range(tiles):
                    turned[i, c, pl.ds(g, LANES, stride=tiles), :] = v[g * LANES : (g + 1) * LANES]
            out[0, slot] = jnp.concatenate([turned[i, c] for c in range(4)], 1).astype(BF)
        return 0

    lax.fori_loop(0, slots // GROUP, some_slots, 0)


def pairs(block, count, partner, low, high, strips, edges):
    dates, rows, cols = strips[0].shape
    slots = partner.shape[1]
    tables = constants(cols // 2, rows)
    scalars = pl.BlockSpec(memory_space=pltpu.SMEM)
    whole = pl.BlockSpec(memory_space=pltpu.VMEM)
    blocks = len(strips)
    return pl.pallas_call(
        functools.partial(pairs_kernel, blocks=blocks),
        grid=(dates,),
        in_specs=[scalars] * 5 + [whole] * (2 * blocks + len(tables)),
        out_specs=pl.BlockSpec((1, slots, rows, cols), lambda d: (d, 0, 0, 0)),
        out_shape=jax.ShapeDtypeStruct((dates, slots, rows, cols), BF),
        scratch_shapes=[
            pltpu.VMEM((blocks * dates, rows + 2 * LANES, cols), BF),
            pltpu.VMEM((GROUP, 4, rows, cols // 4), F32),
        ],
        compiler_params=pltpu.CompilerParams(vmem_limit_bytes=48 * 2**20),
    )(block, count, partner, low, high, *strips, *edges, *tables)


def local(acquisitions, partner, pair_count, band_low, band_high):
    blocks = lax.axis_size("date")
    strips_count = lax.axis_size("space")
    up = [(i, i + 1) for i in range(strips_count - 1)]
    down = [(i + 1, i) for i in range(strips_count - 1)]
    before = lax.ppermute(acquisitions[:, -1, :], "space", up)
    after = lax.ppermute(acquisitions[:, 0, :], "space", down)
    edge = jnp.concatenate([before, after], 0)

    def from_ahead(x, k):
        return lax.ppermute(x, "date", [((i + k) % blocks, i) for i in range(blocks)]) if k else x

    strips = [from_ahead(acquisitions, k) for k in range(blocks)]
    edges = [from_ahead(edge, k) for k in range(blocks)]
    block = lax.axis_index("date").reshape(1).astype(jnp.int32)
    return pairs(block, pair_count, partner, band_low, band_high, strips, edges)


def solution(mesh):
    placed = (P("date", "space", None), P(), P(), P("date", None), P("date", None))
    return jax.shard_map(
        local, mesh=mesh, in_specs=placed, out_specs=P("date", None, "space", None), check_vma=False
    )
```

```python
import functools

import jax
import jax.numpy as jnp
import ml_dtypes
import numpy as np
from jax import lax
from jax.experimental import pallas as pl
from jax.experimental.pallas import tpu as pltpu
from jax.sharding import PartitionSpec as P

BF = jnp.bfloat16
F32 = jnp.float32
TILE = 16
SUB = 8


def constants(bins):
    k = np.arange(bins)
    angle = (k[:, None] * k[None, :] % bins) * (2.0 * np.pi / bins)
    cosine, sine = np.cos(angle), np.sin(angle)
    forward = np.block([[cosine, -sine], [sine, cosine]])
    inverse = np.block([[cosine, sine], [-sine, cosine]]) / bins
    half = bins // 2
    even, odd = np.arange(0, bins, 2), np.arange(1, bins, 2)
    even, odd = np.concatenate([even, bins + even]), np.concatenate([odd, bins + odd])
    first = np.concatenate([np.arange(half), bins + np.arange(half)])
    band = np.abs(k[:, None] - k[None, :]) <= 4
    made = (forward[:, np.concatenate([even, odd])], inverse[even][:, first], inverse[odd][:, first], band)
    return [jnp.asarray(m.astype(np.float32).astype(ml_dtypes.bfloat16)) for m in made]


def dot(a, b):
    return lax.dot_general(a, b, (((1,), (0,)), ((), ())), preferred_element_type=F32)


def pairs_kernel(block, count, partner, low, high, *refs, blocks):
    mains, edges, refs = refs[:blocks], refs[blocks : 2 * blocks], refs[2 * blocks :]
    forward, inv_even, inv_odd, band, out = refs[:5]
    spectra, sums, across, ready, main_sem, out_sem = refs[5:]
    dates, slots = low.shape
    ext, cols = spectra.shape[1:]
    rows = ext - TILE
    bins = cols // 2
    half = bins // 2
    here = block[0]

    def main_copy(k):
        place = spectra.at[pl.ds(k * dates, dates), pl.ds(0, rows)]
        return pltpu.make_async_copy(mains[k], place, main_sem.at[k])

    for k in range(blocks):
        main_copy(k).start()

    tile_row = lax.broadcasted_iota(jnp.int32, (TILE, cols), 0)
    for k in range(blocks):
        edge = dot(edges[k][...], forward[...]).astype(BF).astype(F32)
        for q in range(dates):
            before, after = edge[q : q + 1], edge[dates + q : dates + q + 1]
            tile = jnp.where(tile_row == 0, after, jnp.where(tile_row == TILE - 1, before, 0.0))
            spectra[k * dates + q, rows:ext] = tile.astype(BF)

    lane = lax.broadcasted_iota(jnp.int32, (TILE, cols), 1)
    bin_id = lane % half * 2 + lane // bins
    even, odd, window = inv_even[...], inv_odd[...], band[...]

    def masked(date, slot):
        whole_date = here * dates + date
        live = slot < count[whole_date]
        low_bin = jnp.where(live, low[date, slot], 0)
        high_bin = jnp.where(live, high[date, slot], 0)
        mask = jnp.where((bin_id >= low_bin) & (bin_id < high_bin), 1.0, 0.0).astype(BF)[None]
        second = partner[whole_date, slot]
        away = second // dates - here
        away = jnp.where(away < 0, away + blocks, away)
        tiled = (ext // TILE, TILE, cols)
        a = (spectra[date].reshape(tiled) * mask).reshape(ext, cols)
        b = (spectra[away * dates + second % dates].reshape(tiled) * mask).reshape(ext, cols)
        return [a, b]

    def filter_date(date, ring):
        x = jnp.concatenate([m for slot in range(slots) for m in masked(date, slot)], 0)
        e = dot(x[:, :bins], even)
        o = dot(x[:, bins:], odd)
        for slot in range(slots):
            r = slice(2 * slot * ext, (2 * slot + 2) * ext)
            for c, v in enumerate(((e[r] + o[r]).astype(BF), (e[r] - o[r]).astype(BF))):
                a_re, a_im, b_re, b_im = v[:ext, :half], v[:ext, half:], v[ext:, :half], v[ext:, half:]
                fields = (
                    a_re * b_re + a_im * b_im,
                    a_im * b_re - a_re * b_im,
                    a_re * a_re + a_im * a_im,
                    b_re * b_re + b_im * b_im,
                )
                for q, field in enumerate(fields):
                    sums[ring, slot, q * ext : (q + 1) * ext, c * half : (c + 1) * half] = field

    def look_date(ring):
        cut = slots // 2
        groups = [list(range(cut)), list(range(cut, slots))]
        summed = []
        for group in groups:
            if group:
                y = dot(jnp.concatenate([sums[ring, slot] for slot in group], 0), window)
                summed += [y[4 * i * ext : 4 * (i + 1) * ext] for i in range(len(group))]
        for slot in range(slots):
            looked = []
            for q in range(4):
                parts = []
                for c in range(2):
                    v = summed[slot][q * ext : (q + 1) * ext, c * half : (c + 1) * half]
                    held = across.at[slot, 2 * q + c]
                    held[0:SUB] = v[ext - SUB :]
                    held[SUB:ext] = v[: ext - SUB]
                    parts.append(
                        held[SUB - 1 : SUB - 1 + rows] + held[SUB : SUB + rows] + held[SUB + 1 : SUB + 1 + rows]
                    )
                looked.append(jnp.concatenate(parts, 1))
            scale = lax.rsqrt(jnp.maximum(looked[2], 1.0) * jnp.maximum(looked[3], 1.0))
            ready[ring, slot, :, :bins] = (looked[0] * scale).astype(BF)
            ready[ring, slot, :, bins:] = (looked[1] * scale).astype(BF)

    def send(date, ring):
        return pltpu.make_async_copy(ready.at[ring], out.at[date], out_sem.at[ring])

    for k in range(blocks):
        main_copy(k).wait()
    filter_date(0, 0)

    def body(date, _):
        now = lax.rem(date, 2)
        last = 1 - now

        @pl.when(date >= 3)
        def _():
            send(date - 3, last).wait()

        look_date(last)
        filter_date(date, now)
        send(date - 1, last).start()
        return 0

    lax.fori_loop(1, dates, body, 0)
    end = (dates - 1) % 2
    if dates >= 3:
        send(dates - 3, end).wait()
    look_date(end)
    send(dates - 1, end).start()
    if dates >= 2:
        send(dates - 2, 1 - end).wait()
    send(dates - 1, end).wait()


def pairs(block, count, partner, low, high, mains, edges, tables):
    dates, rows, cols = mains[0].shape
    slots = partner.shape[1]
    ext = rows + TILE
    scalars = pl.BlockSpec(memory_space=pltpu.SMEM)
    whole = pl.BlockSpec(memory_space=pltpu.VMEM)
    anywhere = pl.BlockSpec(memory_space=pl.ANY)
    blocks = len(mains)
    work = dates * slots * rows * cols
    return pl.pallas_call(
        functools.partial(pairs_kernel, blocks=blocks),
        in_specs=[scalars] * 5 + [anywhere] * blocks + [whole] * (blocks + len(tables)),
        out_specs=anywhere,
        out_shape=jax.ShapeDtypeStruct((dates, slots, rows, cols), BF),
        scratch_shapes=[
            pltpu.VMEM((blocks * dates, ext, cols), BF),
            pltpu.VMEM((2, slots, 4 * ext, cols // 2), BF),
            pltpu.VMEM((slots, 8, ext, cols // 4), F32),
            pltpu.VMEM((2, slots, rows, cols), BF),
            pltpu.SemaphoreType.DMA((blocks,)),
            pltpu.SemaphoreType.DMA((2,)),
        ],
        cost_estimate=pl.CostEstimate(flops=work * cols * 4, bytes_accessed=work * 2, transcendentals=work // 2),
        compiler_params=pltpu.CompilerParams(vmem_limit_bytes=58 * 2**20),
    )(block, count, partner, low, high, *mains, *edges, *tables)


def edge_rows(strips):
    n = lax.axis_size("space")
    even = lax.axis_index("space") % 2 == 0
    first, last = strips[:, 0, :], strips[:, -1, :]
    inner = [(i, i ^ 1) for i in range(n) if i ^ 1 < n]
    outer = [(i, i + 1) for i in range(1, n - 1, 2)] + [(i + 1, i) for i in range(1, n - 1, 2)]
    from_inner = lax.ppermute(jnp.where(even, last, first), "space", inner)
    from_outer = lax.ppermute(jnp.where(even, first, last), "space", outer)
    return jnp.concatenate([jnp.where(even, from_outer, from_inner), jnp.where(even, from_inner, from_outer)], 0)


def local(acquisitions, partner, pair_count, band_low, band_high):
    blocks = lax.axis_size("date")
    dates, rows, cols = acquisitions.shape
    tables = constants(cols // 2)

    def from_ahead(x, k):
        return lax.ppermute(x, "date", [((i + k) % blocks, i) for i in range(blocks)]) if k else x

    edge = edge_rows(acquisitions)
    mains = []
    for k in range(blocks):
        strip = from_ahead(acquisitions, k).reshape(dates * rows, cols)
        spectrum = jnp.dot(strip, tables[0], preferred_element_type=F32).astype(BF)
        mains.append(spectrum.reshape(dates, rows, cols))
    edges = [from_ahead(edge, k) for k in range(blocks)]
    block = lax.axis_index("date").reshape(1).astype(jnp.int32)
    return pairs(block, pair_count, partner, band_low, band_high, mains, edges, tables)


def solution(mesh):
    placed = (P("date", "space", None), P(), P(), P("date", None), P("date", None))
    return jax.shard_map(
        local, mesh=mesh, in_specs=placed, out_specs=P("date", None, "space", None), check_vma=False
    )
```

```python
import functools

import jax
import jax.numpy as jnp
import ml_dtypes
import numpy as np
from jax import lax
from jax.experimental import pallas as pl
from jax.experimental.layout import Layout, with_layout_constraint
from jax.experimental.pallas import tpu as pltpu
from jax.sharding import PartitionSpec as P

BF = jnp.bfloat16
F32 = jnp.float32
TILE = 16
SUB = 8


def constants(bins):
    k = np.arange(bins)
    angle = (k[:, None] * k[None, :] % bins) * (2.0 * np.pi / bins)
    cosine, sine = np.cos(angle), np.sin(angle)
    forward = np.block([[cosine, -sine], [sine, cosine]])
    inverse = np.block([[cosine, sine], [-sine, cosine]]) / bins
    half = bins // 2
    even, odd = np.arange(0, bins, 2), np.arange(1, bins, 2)
    even, odd = np.concatenate([even, bins + even]), np.concatenate([odd, bins + odd])
    first = np.concatenate([np.arange(half), bins + np.arange(half)])
    band = np.abs(k[:, None] - k[None, :]) <= 4
    made = (forward[:, np.concatenate([even, odd])], inverse[even][:, first], inverse[odd][:, first], band)
    return [jnp.asarray(m.astype(np.float32).astype(ml_dtypes.bfloat16)) for m in made]


def dot(a, b):
    return lax.dot_general(a, b, (((1,), (0,)), ((), ())), preferred_element_type=F32)


def pairs_kernel(block, count, partner, low, high, *refs, blocks):
    mains, edges, refs = refs[:blocks], refs[blocks : 2 * blocks], refs[2 * blocks :]
    forward, inv_even, inv_odd, band, out = refs[:5]
    spectra, sums, across, ready, main_sem, out_sem = refs[5:]
    dates, slots = low.shape
    ext, cols = spectra.shape[1:]
    rows = ext - TILE
    bins = cols // 2
    half = bins // 2
    here = block[0]

    def main_copy(k):
        place = spectra.at[pl.ds(k * dates, dates), pl.ds(0, rows)]
        return pltpu.make_async_copy(mains[k], place, main_sem.at[k])

    for k in range(blocks):
        main_copy(k).start()

    tile_row = lax.broadcasted_iota(jnp.int32, (TILE, cols), 0)
    for k in range(blocks):
        edge = dot(edges[k][...], forward[...]).astype(BF).astype(F32)
        for q in range(dates):
            before, after = edge[q : q + 1], edge[dates + q : dates + q + 1]
            tile = jnp.where(tile_row == 0, after, jnp.where(tile_row == TILE - 1, before, 0.0))
            spectra[k * dates + q, rows:ext] = tile.astype(BF)

    lane = lax.broadcasted_iota(jnp.int32, (TILE, cols), 1)
    bin_id = lane % half * 2 + lane // bins
    even, odd, window = inv_even[...], inv_odd[...], band[...]

    def masked(date, slot):
        whole_date = here * dates + date
        live = slot < count[whole_date]
        low_bin = jnp.where(live, low[date, slot], 0)
        high_bin = jnp.where(live, high[date, slot], 0)
        mask = jnp.where((bin_id >= low_bin) & (bin_id < high_bin), 1.0, 0.0).astype(BF)[None]
        second = partner[whole_date, slot]
        away = second // dates - here
        away = jnp.where(away < 0, away + blocks, away)
        tiled = (ext // TILE, TILE, cols)
        a = (spectra[date].reshape(tiled) * mask).reshape(ext, cols)
        b = (spectra[away * dates + second % dates].reshape(tiled) * mask).reshape(ext, cols)
        return [a, b]

    def filter_date(date, ring, group):
        x = jnp.concatenate([m for slot in group for m in masked(date, slot)], 0)
        e = dot(x[:, :bins], even)
        o = dot(x[:, bins:], odd)
        for i, slot in enumerate(group):
            r = slice(2 * i * ext, (2 * i + 2) * ext)
            for c, v in enumerate(((e[r] + o[r]).astype(BF), (e[r] - o[r]).astype(BF))):
                a_re, a_im, b_re, b_im = v[:ext, :half], v[:ext, half:], v[ext:, :half], v[ext:, half:]
                fields = (
                    a_re * b_re + a_im * b_im,
                    a_im * b_re - a_re * b_im,
                    a_re * a_re + a_im * a_im,
                    b_re * b_re + b_im * b_im,
                )
                for q, field in enumerate(fields):
                    sums[ring, slot, q * ext : (q + 1) * ext, c * half : (c + 1) * half] = field

    def look_date(ring, group):
        flat = jnp.concatenate([sums[ring, slot] for slot in group], 0)
        cut = flat.shape[0] // (2 * TILE) * TILE
        summed = jnp.concatenate([dot(flat[:cut], window), dot(flat[cut:], window)], 0)
        for i, slot in enumerate(group):
            looked = []
            for q in range(4):
                parts = []
                for c in range(2):
                    v = summed[(4 * i + q) * ext : (4 * i + q + 1) * ext, c * half : (c + 1) * half]
                    held = across.at[slot, 2 * q + c]
                    held[0:SUB] = v[ext - SUB :]
                    held[SUB:ext] = v[: ext - SUB]
                    parts.append(
                        held[SUB - 1 : SUB - 1 + rows] + v[:rows] + held[SUB + 1 : SUB + 1 + rows]
                    )
                looked.append(jnp.concatenate(parts, 1))
            scale = lax.rsqrt(jnp.maximum(looked[2], 1.0) * jnp.maximum(looked[3], 1.0))
            ready[ring, slot, :, :bins] = (looked[0] * scale).astype(BF)
            ready[ring, slot, :, bins:] = (looked[1] * scale).astype(BF)

    def send(date, ring):
        return pltpu.make_async_copy(ready.at[ring], out.at[date], out_sem.at[ring])

    for k in range(blocks):
        main_copy(k).wait()
    parts_of_date = 1
    groups = [list(range(slots * g // parts_of_date, slots * (g + 1) // parts_of_date)) for g in range(parts_of_date)]
    groups = [g for g in groups if g]
    for group in groups:
        filter_date(0, 0, group)

    def body(date, _):
        now = lax.rem(date, 2)
        last = 1 - now

        @pl.when(date >= 3)
        def _():
            send(date - 3, last).wait()

        for group in groups:
            look_date(last, group)
            filter_date(date, now, group)
        send(date - 1, last).start()
        return 0

    lax.fori_loop(1, dates, body, 0)
    end = (dates - 1) % 2
    if dates >= 3:
        send(dates - 3, end).wait()
    for group in groups:
        look_date(end, group)
    send(dates - 1, end).start()
    if dates >= 2:
        send(dates - 2, 1 - end).wait()
    send(dates - 1, end).wait()


def pairs(block, count, partner, low, high, mains, edges, tables):
    dates, rows, cols = mains[0].shape
    slots = partner.shape[1]
    ext = rows + TILE
    scalars = pl.BlockSpec(memory_space=pltpu.SMEM)
    whole = pl.BlockSpec(memory_space=pltpu.VMEM)
    anywhere = pl.BlockSpec(memory_space=pl.ANY)
    blocks = len(mains)
    work = dates * slots * rows * cols
    return pl.pallas_call(
        functools.partial(pairs_kernel, blocks=blocks),
        in_specs=[scalars] * 5 + [anywhere] * blocks + [whole] * (blocks + len(tables)),
        out_specs=anywhere,
        out_shape=jax.ShapeDtypeStruct((dates, slots, rows, cols), BF),
        scratch_shapes=[
            pltpu.VMEM((blocks * dates, ext, cols), BF),
            pltpu.VMEM((2, slots, 4 * ext, cols // 2), BF),
            pltpu.VMEM((slots, 8, ext, cols // 4), F32),
            pltpu.VMEM((2, slots, rows, cols), BF),
            pltpu.SemaphoreType.DMA((blocks,)),
            pltpu.SemaphoreType.DMA((2,)),
        ],
        cost_estimate=pl.CostEstimate(flops=work * cols * 4, bytes_accessed=work * 2, transcendentals=work // 2),
        compiler_params=pltpu.CompilerParams(vmem_limit_bytes=53 * 2**20),
    )(block, count, partner, low, high, *mains, *edges, *tables)


def edge_rows(strips):
    n = lax.axis_size("space")
    even = lax.axis_index("space") % 2 == 0
    first, last = strips[:, 0, :], strips[:, -1, :]
    inner = [(i, i ^ 1) for i in range(n) if i ^ 1 < n]
    outer = [(i, i + 1) for i in range(1, n - 1, 2)] + [(i + 1, i) for i in range(1, n - 1, 2)]
    from_inner = lax.ppermute(jnp.where(even, last, first), "space", inner)
    from_outer = lax.ppermute(jnp.where(even, first, last), "space", outer)
    return jnp.concatenate([jnp.where(even, from_outer, from_inner), jnp.where(even, from_inner, from_outer)], 0)


def local(acquisitions, partner, pair_count, band_low, band_high):
    blocks = lax.axis_size("date")
    dates, rows, cols = acquisitions.shape
    tables = constants(cols // 2)

    def from_ahead(x, k):
        return lax.ppermute(x, "date", [((i + k) % blocks, i) for i in range(blocks)]) if k else x

    edge = edge_rows(acquisitions)
    mains = []
    for k in range(blocks):
        strip = from_ahead(acquisitions, k).reshape(dates * rows, cols)
        spectrum = jnp.dot(strip, tables[0], preferred_element_type=F32).astype(BF)
        spectrum = with_layout_constraint(spectrum, Layout(major_to_minor=(0, 1)))
        mains.append(spectrum.reshape(dates, rows, cols))
    edges = [from_ahead(edge, k) for k in range(blocks)]
    block = lax.axis_index("date").reshape(1).astype(jnp.int32)
    return pairs(block, pair_count, partner, band_low, band_high, mains, edges, tables)


def solution(mesh):
    placed = (P("date", "space", None), P(), P(), P("date", None), P("date", None))
    return jax.shard_map(
        local, mesh=mesh, in_specs=placed, out_specs=P("date", None, "space", None), check_vma=False
    )
```

```python
import functools

import jax
import jax.numpy as jnp
import ml_dtypes
import numpy as np
from jax import lax
from jax.experimental import pallas as pl
from jax.experimental.layout import Layout, with_layout_constraint
from jax.experimental.pallas import tpu as pltpu
from jax.sharding import PartitionSpec as P

BF = jnp.bfloat16
F32 = jnp.float32
TILE = 16
SUB = 8


def constants(bins):
    k = np.arange(bins)
    angle = (k[:, None] * k[None, :] % bins) * (2.0 * np.pi / bins)
    cosine, sine = np.cos(angle), np.sin(angle)
    forward = np.block([[cosine, -sine], [sine, cosine]])
    inverse = np.block([[cosine, sine], [-sine, cosine]]) / bins
    half = bins // 2
    even, odd = np.arange(0, bins, 2), np.arange(1, bins, 2)
    even, odd = np.concatenate([even, bins + even]), np.concatenate([odd, bins + odd])
    first = np.concatenate([np.arange(half), bins + np.arange(half)])
    band = np.abs(k[:, None] - k[None, :]) <= 4
    made = (forward[:, np.concatenate([even, odd])], inverse[even][:, first], inverse[odd][:, first], band)
    return [jnp.asarray(m.astype(np.float32).astype(ml_dtypes.bfloat16)) for m in made]


def dot(a, b):
    return lax.dot_general(a, b, (((1,), (0,)), ((), ())), preferred_element_type=F32)


def pairs_kernel(block, count, partner, low, high, *refs, blocks):
    mains, edges, refs = refs[:blocks], refs[blocks : 2 * blocks], refs[2 * blocks :]
    forward, inv_even, inv_odd, band, out = refs[:5]
    spectra, sums, across, ready, main_sem, out_sem = refs[5:]
    dates, slots = low.shape
    ext, cols = spectra.shape[1:]
    rows = ext - TILE
    bins = cols // 2
    half = bins // 2
    here = block[0]

    def main_copy(k, first, last, sem):
        place = spectra.at[pl.ds(k * dates + first, last - first), pl.ds(0, rows)]
        return pltpu.make_async_copy(mains[k].at[pl.ds(first, last - first)], place, main_sem.at[sem])

    early = [main_copy(k, 0, dates, k) for k in range(1, blocks)] + [main_copy(0, 0, 1, 0)]
    later = [main_copy(0, 1, dates, blocks)] if dates > 1 else []
    for copy in early + later:
        copy.start()

    tile_row = lax.broadcasted_iota(jnp.int32, (TILE, cols), 0)
    for k in range(blocks):
        edge = dot(edges[k][...], forward[...]).astype(BF).astype(F32)
        for q in range(dates):
            before, after = edge[q : q + 1], edge[dates + q : dates + q + 1]
            tile = jnp.where(tile_row == 0, after, jnp.where(tile_row == TILE - 1, before, 0.0))
            spectra[k * dates + q, rows:ext] = tile.astype(BF)

    lane = lax.broadcasted_iota(jnp.int32, (TILE, cols), 1)
    bin_id = lane % half * 2 + lane // bins
    even, odd, window = inv_even[...], inv_odd[...], band[...]

    def masked(date, slot):
        whole_date = here * dates + date
        live = slot < count[whole_date]
        low_bin = jnp.where(live, low[date, slot], 0)
        high_bin = jnp.where(live, high[date, slot], 0)
        mask = jnp.where((bin_id >= low_bin) & (bin_id < high_bin), 1.0, 0.0).astype(BF)[None]
        second = partner[whole_date, slot]
        away = second // dates - here
        away = jnp.where(away < 0, away + blocks, away)
        tiled = (ext // TILE, TILE, cols)
        a = (spectra[date].reshape(tiled) * mask).reshape(ext, cols)
        b = (spectra[away * dates + second % dates].reshape(tiled) * mask).reshape(ext, cols)
        return [a, b]

    def filter_date(date, ring, group):
        x = jnp.concatenate([m for slot in group for m in masked(date, slot)], 0)
        e = dot(x[:, :bins], even)
        o = dot(x[:, bins:], odd)
        for i, slot in enumerate(group):
            r = slice(2 * i * ext, (2 * i + 2) * ext)
            for c, v in enumerate(((e[r] + o[r]).astype(BF), (e[r] - o[r]).astype(BF))):
                a_re, a_im, b_re, b_im = v[:ext, :half], v[:ext, half:], v[ext:, :half], v[ext:, half:]
                fields = (
                    a_re * b_re + a_im * b_im,
                    a_im * b_re - a_re * b_im,
                    a_re * a_re + a_im * a_im,
                    b_re * b_re + b_im * b_im,
                )
                for q, field in enumerate(fields):
                    sums[ring, slot, q * ext : (q + 1) * ext, c * half : (c + 1) * half] = field

    def look_date(ring, group, then=None):
        flat = jnp.concatenate([sums[ring, slot] for slot in group], 0)
        cut = flat.shape[0] // (2 * TILE) * TILE
        summed = jnp.concatenate([dot(flat[:cut], window), dot(flat[cut:], window)], 0)
        for i, slot in enumerate(group):
            looked = []
            for q in range(4):
                parts = []
                for c in range(2):
                    v = summed[(4 * i + q) * ext : (4 * i + q + 1) * ext, c * half : (c + 1) * half]
                    held = across.at[slot, 2 * q + c]
                    held[0:SUB] = v[ext - SUB :]
                    held[SUB:ext] = v[: ext - SUB]
                    parts.append(
                        held[SUB - 1 : SUB - 1 + rows] + v[:rows] + held[SUB + 1 : SUB + 1 + rows]
                    )
                looked.append(jnp.concatenate(parts, 1))
            scale = lax.rsqrt(jnp.maximum(looked[2], 1.0) * jnp.maximum(looked[3], 1.0))
            ready[ring, slot, :, :bins] = (looked[0] * scale).astype(BF)
            ready[ring, slot, :, bins:] = (looked[1] * scale).astype(BF)
            if then is not None:
                then(slot)

    def send(date, ring):
        return pltpu.make_async_copy(ready.at[ring], out.at[date], out_sem.at[ring])

    for copy in early:
        copy.wait()
    parts_of_date = 1
    groups = [list(range(slots * g // parts_of_date, slots * (g + 1) // parts_of_date)) for g in range(parts_of_date)]
    groups = [g for g in groups if g]
    for group in groups:
        filter_date(0, 0, group)
    for copy in later:
        copy.wait()

    def body(date, _):
        now = lax.rem(date, 2)
        last = 1 - now

        @pl.when(date >= 3)
        def _():
            send(date - 3, last).wait()

        for group in groups:
            look_date(last, group)
            filter_date(date, now, group)
        send(date - 1, last).start()
        return 0

    lax.fori_loop(1, dates, body, 0)
    end = (dates - 1) % 2

    def send_slot(slot):
        pltpu.make_async_copy(ready.at[end, slot], out.at[dates - 1, slot], out_sem.at[end]).start()

    if dates >= 3:
        send(dates - 3, end).wait()
    for group in groups:
        look_date(end, group, send_slot)
    if dates >= 2:
        send(dates - 2, 1 - end).wait()
    send(dates - 1, end).wait()


def pairs(block, count, partner, low, high, mains, edges, tables):
    dates, rows, cols = mains[0].shape
    slots = partner.shape[1]
    ext = rows + TILE
    scalars = pl.BlockSpec(memory_space=pltpu.SMEM)
    whole = pl.BlockSpec(memory_space=pltpu.VMEM)
    anywhere = pl.BlockSpec(memory_space=pl.ANY)
    blocks = len(mains)
    work = dates * slots * rows * cols
    return pl.pallas_call(
        functools.partial(pairs_kernel, blocks=blocks),
        in_specs=[scalars] * 5 + [anywhere] * blocks + [whole] * (blocks + len(tables)),
        out_specs=anywhere,
        out_shape=jax.ShapeDtypeStruct((dates, slots, rows, cols), BF),
        scratch_shapes=[
            pltpu.VMEM((blocks * dates, ext, cols), BF),
            pltpu.VMEM((2, slots, 4 * ext, cols // 2), BF),
            pltpu.VMEM((slots, 8, ext, cols // 4), F32),
            pltpu.VMEM((2, slots, rows, cols), BF),
            pltpu.SemaphoreType.DMA((blocks + 1,)),
            pltpu.SemaphoreType.DMA((2,)),
        ],
        cost_estimate=pl.CostEstimate(flops=work * cols * 4, bytes_accessed=work * 2, transcendentals=work // 2),
        compiler_params=pltpu.CompilerParams(vmem_limit_bytes=53 * 2**20),
    )(block, count, partner, low, high, *mains, *edges, *tables)


def edge_rows(strips):
    n = lax.axis_size("space")
    even = lax.axis_index("space") % 2 == 0
    first, last = strips[:, 0, :], strips[:, -1, :]
    inner = [(i, i ^ 1) for i in range(n) if i ^ 1 < n]
    outer = [(i, i + 1) for i in range(1, n - 1, 2)] + [(i + 1, i) for i in range(1, n - 1, 2)]
    from_inner = lax.ppermute(jnp.where(even, last, first), "space", inner)
    from_outer = lax.ppermute(jnp.where(even, first, last), "space", outer)
    odd = jnp.logical_not(even)
    return jnp.concatenate([jnp.where(odd, from_inner, from_outer), jnp.where(odd, from_outer, from_inner)], 0)


def local(acquisitions, partner, pair_count, band_low, band_high):
    blocks = lax.axis_size("date")
    dates, rows, cols = acquisitions.shape
    tables = constants(cols // 2)

    def from_ahead(x, k):
        return lax.ppermute(x, "date", [((i + k) % blocks, i) for i in range(blocks)]) if k else x

    edge = edge_rows(acquisitions)
    mains = []
    for k in range(blocks):
        strip = from_ahead(acquisitions, k).reshape(dates * rows, cols)
        spectrum = jnp.dot(strip, tables[0], preferred_element_type=F32).astype(BF)
        spectrum = with_layout_constraint(spectrum, Layout(major_to_minor=(0, 1)))
        mains.append(spectrum.reshape(dates, rows, cols))
    edges = [from_ahead(edge, k) for k in range(blocks)]
    block = lax.axis_index("date").reshape(1).astype(jnp.int32)
    return pairs(block, pair_count, partner, band_low, band_high, mains, edges, tables)


def solution(mesh):
    placed = (P("date", "space", None), P(), P(), P("date", None), P("date", None))
    return jax.shard_map(
        local, mesh=mesh, in_specs=placed, out_specs=P("date", None, "space", None), check_vma=False
    )
```

```python
import functools

import jax
import jax.numpy as jnp
import ml_dtypes
import numpy as np
from jax import lax
from jax.experimental import pallas as pl
from jax.experimental.layout import Layout, with_layout_constraint
from jax.experimental.pallas import tpu as pltpu
from jax.sharding import PartitionSpec as P

BF = jnp.bfloat16
F32 = jnp.float32
TILE = 16
SUB = 8


def constants(bins):
    k = np.arange(bins)
    angle = (k[:, None] * k[None, :] % bins) * (2.0 * np.pi / bins)
    cosine, sine = np.cos(angle), np.sin(angle)
    forward = np.block([[cosine, -sine], [sine, cosine]])
    inverse = np.block([[cosine, sine], [-sine, cosine]]) / bins
    half = bins // 2
    even, odd = np.arange(0, bins, 2), np.arange(1, bins, 2)
    even, odd = np.concatenate([even, bins + even]), np.concatenate([odd, bins + odd])
    first = np.concatenate([np.arange(half), bins + np.arange(half)])
    band = np.abs(k[:, None] - k[None, :]) <= 4
    made = (forward[:, np.concatenate([even, odd])], inverse[even][:, first], inverse[odd][:, first], band)
    return [jnp.asarray(m.astype(np.float32).astype(ml_dtypes.bfloat16)) for m in made]


def dot(a, b):
    return lax.dot_general(a, b, (((1,), (0,)), ((), ())), preferred_element_type=F32)


def pairs_kernel(block, count, partner, low, high, *refs, blocks):
    mains, edges, refs = refs[:blocks], refs[blocks : 2 * blocks], refs[2 * blocks :]
    forward, inv_even, inv_odd, band, out = refs[:5]
    spectra, sums, across, ready, main_sem, out_sem = refs[5:]
    dates, slots = low.shape
    ext, cols = spectra.shape[1:]
    rows = ext - TILE
    bins = cols // 2
    half = bins // 2
    here = block[0]

    def main_copy(k, first, last, sem):
        place = spectra.at[pl.ds(k * dates + first, last - first), pl.ds(0, rows)]
        return pltpu.make_async_copy(mains[k].at[pl.ds(first, last - first)], place, main_sem.at[sem])

    early = [main_copy(k, 0, dates, k) for k in range(1, blocks)] + [main_copy(0, 0, 1, 0)]
    later = [main_copy(0, 1, dates, blocks)] if dates > 1 else []
    for copy in early + later:
        copy.start()

    tile_row = lax.broadcasted_iota(jnp.int32, (TILE, cols), 0)
    for k in range(blocks):
        edge = dot(edges[k][...], forward[...]).astype(BF).astype(F32)
        for q in range(dates):
            before, after = edge[q : q + 1], edge[dates + q : dates + q + 1]
            tile = jnp.where(tile_row == 0, after, jnp.where(tile_row == TILE - 1, before, 0.0))
            spectra[k * dates + q, rows:ext] = tile.astype(BF)

    lane = lax.broadcasted_iota(jnp.int32, (TILE, cols), 1)
    bin_id = lane % half * 2 + lane // bins
    even, odd, window = inv_even[...], inv_odd[...], band[...]

    def masked(date, slot):
        whole_date = here * dates + date
        live = slot < count[whole_date]
        low_bin = jnp.where(live, low[date, slot], 0)
        high_bin = jnp.where(live, high[date, slot], 0)
        mask = jnp.where((bin_id >= low_bin) & (bin_id < high_bin), 1.0, 0.0).astype(BF)[None]
        second = partner[whole_date, slot]
        away = second // dates - here
        away = jnp.where(away < 0, away + blocks, away)
        tiled = (ext // TILE, TILE, cols)
        a = (spectra[date].reshape(tiled) * mask).reshape(ext, cols)
        b = (spectra[away * dates + second % dates].reshape(tiled) * mask).reshape(ext, cols)
        return [a, b]

    def filter_date(date, ring, group):
        x = jnp.concatenate([m for slot in group for m in masked(date, slot)], 0)
        e = dot(x[:, :bins], even)
        o = dot(x[:, bins:], odd)
        for i, slot in enumerate(group):
            r = slice(2 * i * ext, (2 * i + 2) * ext)
            for c, v in enumerate(((e[r] + o[r]).astype(BF), (e[r] - o[r]).astype(BF))):
                a_re, a_im, b_re, b_im = v[:ext, :half], v[:ext, half:], v[ext:, :half], v[ext:, half:]
                fields = (
                    a_re * b_re + a_im * b_im,
                    a_im * b_re - a_re * b_im,
                    a_re * a_re + a_im * a_im,
                    b_re * b_re + b_im * b_im,
                )
                for q, field in enumerate(fields):
                    sums[ring, slot, q * ext : (q + 1) * ext, c * half : (c + 1) * half] = field

    def look_date(ring, group, then=None):
        flat = jnp.concatenate([sums[ring, slot] for slot in group], 0)
        cut = flat.shape[0] // (2 * TILE) * TILE
        summed = jnp.concatenate([dot(flat[:cut], window), dot(flat[cut:], window)], 0)
        for i, slot in enumerate(group):
            looked = []
            for q in range(4):
                parts = []
                for c in range(2):
                    v = summed[(4 * i + q) * ext : (4 * i + q + 1) * ext, c * half : (c + 1) * half]
                    held = across.at[slot, 2 * q + c]
                    held[0:SUB] = v[ext - SUB :]
                    held[SUB:ext] = v[: ext - SUB]
                    up = pltpu.roll(v, 1, 0)[:rows] if q < 2 else held[SUB - 1 : SUB - 1 + rows]
                    parts.append(up + v[:rows] + held[SUB + 1 : SUB + 1 + rows])
                looked.append(jnp.concatenate(parts, 1))
            scale = lax.rsqrt(jnp.maximum(looked[2], 1.0) * jnp.maximum(looked[3], 1.0))
            ready[ring, slot, :, :bins] = (looked[0] * scale).astype(BF)
            ready[ring, slot, :, bins:] = (looked[1] * scale).astype(BF)
            if then is not None:
                then(slot)

    def send(date, ring):
        return pltpu.make_async_copy(ready.at[ring], out.at[date], out_sem.at[ring])

    for copy in early:
        copy.wait()
    parts_of_date = 1
    groups = [list(range(slots * g // parts_of_date, slots * (g + 1) // parts_of_date)) for g in range(parts_of_date)]
    groups = [g for g in groups if g]
    for group in groups:
        filter_date(0, 0, group)
    for copy in later:
        copy.wait()

    def body(date, _):
        now = lax.rem(date, 2)
        last = 1 - now

        @pl.when(date >= 3)
        def _():
            send(date - 3, last).wait()

        for group in groups:
            look_date(last, group)
            filter_date(date, now, group)
        send(date - 1, last).start()
        return 0

    lax.fori_loop(1, dates, body, 0)
    end = (dates - 1) % 2

    def send_slot(slot):
        pltpu.make_async_copy(ready.at[end, slot], out.at[dates - 1, slot], out_sem.at[end]).start()

    if dates >= 3:
        send(dates - 3, end).wait()
    for group in groups:
        look_date(end, group, send_slot)
    if dates >= 2:
        send(dates - 2, 1 - end).wait()
    send(dates - 1, end).wait()


def pairs(block, count, partner, low, high, mains, edges, tables):
    dates, rows, cols = mains[0].shape
    slots = partner.shape[1]
    ext = rows + TILE
    scalars = pl.BlockSpec(memory_space=pltpu.SMEM)
    whole = pl.BlockSpec(memory_space=pltpu.VMEM)
    anywhere = pl.BlockSpec(memory_space=pl.ANY)
    blocks = len(mains)
    work = dates * slots * rows * cols
    return pl.pallas_call(
        functools.partial(pairs_kernel, blocks=blocks),
        in_specs=[scalars] * 5 + [anywhere] * blocks + [whole] * (blocks + len(tables)),
        out_specs=anywhere,
        out_shape=jax.ShapeDtypeStruct((dates, slots, rows, cols), BF),
        scratch_shapes=[
            pltpu.VMEM((blocks * dates, ext, cols), BF),
            pltpu.VMEM((2, slots, 4 * ext, cols // 2), BF),
            pltpu.VMEM((slots, 8, ext, cols // 4), F32),
            pltpu.VMEM((2, slots, rows, cols), BF),
            pltpu.SemaphoreType.DMA((blocks + 1,)),
            pltpu.SemaphoreType.DMA((2,)),
        ],
        cost_estimate=pl.CostEstimate(flops=work * cols * 4, bytes_accessed=work * 2, transcendentals=work // 2),
        compiler_params=pltpu.CompilerParams(vmem_limit_bytes=50 * 2**20),
    )(block, count, partner, low, high, *mains, *edges, *tables)


def edge_rows(strips):
    n = lax.axis_size("space")
    even = lax.axis_index("space") % 2 == 0
    first, last = strips[:, 0, :], strips[:, -1, :]
    inner = [(i, i ^ 1) for i in range(n) if i ^ 1 < n]
    outer = [(i, i + 1) for i in range(1, n - 1, 2)] + [(i + 1, i) for i in range(1, n - 1, 2)]
    from_inner = lax.ppermute(jnp.where(even, last, first), "space", inner)
    from_outer = lax.ppermute(jnp.where(even, first, last), "space", outer)
    odd = jnp.logical_not(even)
    return jnp.concatenate([jnp.where(odd, from_inner, from_outer), jnp.where(odd, from_outer, from_inner)], 0)


def local(acquisitions, partner, pair_count, band_low, band_high):
    blocks = lax.axis_size("date")
    dates, rows, cols = acquisitions.shape
    tables = constants(cols // 2)

    def from_ahead(x, k):
        return lax.ppermute(x, "date", [((i + k) % blocks, i) for i in range(blocks)]) if k else x

    edge = edge_rows(acquisitions)
    mains = []
    for k in range(blocks):
        strip = from_ahead(acquisitions, k).reshape(dates * rows, cols)
        spectrum = jnp.dot(strip, tables[0], preferred_element_type=F32).astype(BF)
        spectrum = with_layout_constraint(spectrum, Layout(major_to_minor=(0, 1)))
        mains.append(spectrum.reshape(dates, rows, cols))
    edges = [from_ahead(edge, k) for k in range(blocks)]
    block = lax.axis_index("date").reshape(1).astype(jnp.int32)
    return pairs(block, pair_count, partner, band_low, band_high, mains, edges, tables)


def solution(mesh):
    placed = (P("date", "space", None), P(), P(), P("date", None), P("date", None))
    return jax.shard_map(
        local, mesh=mesh, in_specs=placed, out_specs=P("date", None, "space", None), check_vma=False
    )
```

```python
import functools

import jax
import jax.numpy as jnp
import ml_dtypes
import numpy as np
from jax import lax
from jax.experimental import pallas as pl
from jax.experimental.layout import Layout, with_layout_constraint
from jax.experimental.pallas import tpu as pltpu
from jax.sharding import PartitionSpec as P

BF = jnp.bfloat16
F32 = jnp.float32
TILE = 16
SUB = 8


def constants(bins):
    k = np.arange(bins)
    angle = (k[:, None] * k[None, :] % bins) * (2.0 * np.pi / bins)
    cosine, sine = np.cos(angle), np.sin(angle)
    forward = np.block([[cosine, -sine], [sine, cosine]])
    inverse = np.block([[cosine, sine], [-sine, cosine]]) / bins
    half = bins // 2
    even, odd = np.arange(0, bins, 2), np.arange(1, bins, 2)
    even, odd = np.concatenate([even, bins + even]), np.concatenate([odd, bins + odd])
    first = np.concatenate([np.arange(half), bins + np.arange(half)])
    band = np.abs(k[:, None] - k[None, :]) <= 4
    made = (forward[:, np.concatenate([even, odd])], inverse[even][:, first], inverse[odd][:, first], band)
    return [jnp.asarray(m.astype(np.float32).astype(ml_dtypes.bfloat16)) for m in made]


def dot(a, b):
    return lax.dot_general(a, b, (((1,), (0,)), ((), ())), preferred_element_type=F32)


def pairs_kernel(block, count, partner, low, high, *refs, blocks):
    mains, edges, refs = refs[:blocks], refs[blocks : 2 * blocks], refs[2 * blocks :]
    forward, inv_even, inv_odd, band, out = refs[:5]
    spectra, sums, across, ready, main_sem, out_sem = refs[5:]
    dates, slots = low.shape
    ext, cols = spectra.shape[1:]
    rows = ext - TILE
    bins = cols // 2
    half = bins // 2
    here = block[0]

    def main_copy(k, first, last, sem):
        place = spectra.at[pl.ds(k * dates + first, last - first), pl.ds(0, rows)]
        return pltpu.make_async_copy(mains[k].at[pl.ds(first, last - first)], place, main_sem.at[sem])

    early = [main_copy(k, 0, dates, k) for k in range(1, blocks)] + [main_copy(0, 0, 1, 0)]
    later = [main_copy(0, 1, dates, blocks)] if dates > 1 else []
    for copy in early + later:
        copy.start()

    tile_row = lax.broadcasted_iota(jnp.int32, (TILE, cols), 0)
    for k in range(blocks):
        edge = dot(edges[k][...], forward[...]).astype(BF).astype(F32)
        for q in range(dates):
            before, after = edge[q : q + 1], edge[dates + q : dates + q + 1]
            tile = jnp.where(tile_row == 0, after, jnp.where(tile_row == TILE - 1, before, 0.0))
            spectra[k * dates + q, rows:ext] = tile.astype(BF)

    lane = lax.broadcasted_iota(jnp.int32, (TILE, cols), 1)
    bin_id = lane % half * 2 + lane // bins
    even, odd, window = inv_even[...], inv_odd[...], band[...]

    def masked(date, slot):
        whole_date = here * dates + date
        live = slot < count[whole_date]
        low_bin = jnp.where(live, low[date, slot], 0)
        high_bin = jnp.where(live, high[date, slot], 0)
        mask = jnp.where((bin_id >= low_bin) & (bin_id < high_bin), 1.0, 0.0).astype(BF)[None]
        second = partner[whole_date, slot]
        away = second // dates - here
        away = jnp.where(away < 0, away + blocks, away)
        tiled = (ext // TILE, TILE, cols)
        a = (spectra[date].reshape(tiled) * mask).reshape(ext, cols)
        b = (spectra[away * dates + second % dates].reshape(tiled) * mask).reshape(ext, cols)
        return [a, b]

    def filter_date(date, ring, group):
        x = jnp.concatenate([m for slot in group for m in masked(date, slot)], 0)
        e = dot(x[:, :bins], even)
        o = dot(x[:, bins:], odd)
        for i, slot in enumerate(group):
            r = slice(2 * i * ext, (2 * i + 2) * ext)
            for c, v in enumerate(((e[r] + o[r]).astype(BF), (e[r] - o[r]).astype(BF))):
                a_re, a_im, b_re, b_im = v[:ext, :half], v[:ext, half:], v[ext:, :half], v[ext:, half:]
                fields = (
                    a_re * b_re + a_im * b_im,
                    a_im * b_re - a_re * b_im,
                    a_re * a_re + a_im * a_im,
                    b_re * b_re + b_im * b_im,
                )
                for q, field in enumerate(fields):
                    sums[ring, slot, q * ext : (q + 1) * ext, c * half : (c + 1) * half] = field

    def look_date(ring, group, then=None):
        flat = jnp.concatenate([sums[ring, slot] for slot in group], 0)
        cut = flat.shape[0] // (2 * TILE) * TILE
        summed = jnp.concatenate([dot(flat[:cut], window), dot(flat[cut:], window)], 0)
        for i, slot in enumerate(group):
            looked = []
            for q in range(4):
                parts = []
                for c in range(2):
                    v = summed[(4 * i + q) * ext : (4 * i + q + 1) * ext, c * half : (c + 1) * half]
                    held = across.at[slot, 2 * q + c]
                    held[0:SUB] = v[ext - SUB :]
                    held[SUB:ext] = v[: ext - SUB]
                    up = pltpu.roll(v, 1, 0)[:rows] if q < 2 else held[SUB - 1 : SUB - 1 + rows]
                    parts.append(up + v[:rows] + held[SUB + 1 : SUB + 1 + rows])
                looked.append(jnp.concatenate(parts, 1))
            scale = lax.rsqrt(jnp.maximum(looked[2], 1.0) * jnp.maximum(looked[3], 1.0))
            ready[ring, slot, :, :bins] = (looked[0] * scale).astype(BF)
            ready[ring, slot, :, bins:] = (looked[1] * scale).astype(BF)
            if then is not None:
                then(slot)

    def send(date, ring):
        return pltpu.make_async_copy(ready.at[ring], out.at[date], out_sem.at[ring])

    for copy in early:
        copy.wait()
    parts_of_date = 1
    groups = [list(range(slots * g // parts_of_date, slots * (g + 1) // parts_of_date)) for g in range(parts_of_date)]
    groups = [g for g in groups if g]
    for group in groups:
        filter_date(0, 0, group)
    for copy in later:
        copy.wait()

    def body(date, _):
        now = lax.rem(date, 2)
        last = 1 - now

        @pl.when(date >= 3)
        def _():
            send(date - 3, last).wait()

        for group in groups:
            look_date(last, group)
            filter_date(date, now, group)
        send(date - 1, last).start()
        return 0

    lax.fori_loop(1, dates, body, 0)
    end = (dates - 1) % 2

    def send_slot(slot):
        pltpu.make_async_copy(ready.at[end, slot], out.at[dates - 1, slot], out_sem.at[end]).start()

    if dates >= 3:
        send(dates - 3, end).wait()
    for group in groups:
        look_date(end, group, send_slot)
    if dates >= 2:
        send(dates - 2, 1 - end).wait()
    send(dates - 1, end).wait()


def pairs(block, count, partner, low, high, mains, edges, tables):
    dates, rows, cols = mains[0].shape
    slots = partner.shape[1]
    ext = rows + TILE
    scalars = pl.BlockSpec(memory_space=pltpu.SMEM)
    whole = pl.BlockSpec(memory_space=pltpu.VMEM)
    anywhere = pl.BlockSpec(memory_space=pl.ANY)
    blocks = len(mains)
    work = dates * slots * rows * cols
    return pl.pallas_call(
        functools.partial(pairs_kernel, blocks=blocks),
        in_specs=[scalars] * 5 + [anywhere] * blocks + [whole] * (blocks + len(tables)),
        out_specs=anywhere,
        out_shape=jax.ShapeDtypeStruct((dates, slots, rows, cols), BF),
        scratch_shapes=[
            pltpu.VMEM((blocks * dates, ext, cols), BF),
            pltpu.VMEM((2, slots, 4 * ext, cols // 2), BF),
            pltpu.VMEM((slots, 8, ext, cols // 4), F32),
            pltpu.VMEM((2, slots, rows, cols), BF),
            pltpu.SemaphoreType.DMA((blocks + 1,)),
            pltpu.SemaphoreType.DMA((2,)),
        ],
        cost_estimate=pl.CostEstimate(flops=work * cols * 4, bytes_accessed=work * 2, transcendentals=work // 2),
        compiler_params=pltpu.CompilerParams(vmem_limit_bytes=50 * 2**20),
    )(block, count, partner, low, high, *mains, *edges, *tables)


def edge_rows(strips):
    n = lax.axis_size("space")
    even = lax.axis_index("space") % 2 == 0
    first, last = strips[:, 0, :], strips[:, -1, :]
    inner = [(i, i ^ 1) for i in range(n) if i ^ 1 < n]
    outer = [(i, i + 1) for i in range(1, n - 1, 2)] + [(i + 1, i) for i in range(1, n - 1, 2)]
    from_inner = lax.ppermute(jnp.where(even, last, first), "space", inner)
    from_outer = lax.ppermute(jnp.where(even, first, last), "space", outer)
    return jnp.concatenate([jnp.where(even, from_outer, from_inner), jnp.where(even, from_inner, from_outer)], 0)


def local(acquisitions, partner, pair_count, band_low, band_high):
    blocks = lax.axis_size("date")
    dates, rows, cols = acquisitions.shape
    tables = constants(cols // 2)

    def from_ahead(x, k):
        return lax.ppermute(x, "date", [((i + k) % blocks, i) for i in range(blocks)]) if k else x

    edge = edge_rows(acquisitions)
    mains = []
    for k in range(blocks):
        strip = from_ahead(acquisitions, k).reshape(dates * rows, cols)
        spectrum = jnp.dot(strip, tables[0], preferred_element_type=F32).astype(BF)
        spectrum = with_layout_constraint(spectrum, Layout(major_to_minor=(0, 1)))
        mains.append(spectrum.reshape(dates, rows, cols))
    edges = [from_ahead(edge, k) for k in range(blocks)]
    block = lax.axis_index("date").reshape(1).astype(jnp.int32)
    return pairs(block, pair_count, partner, band_low, band_high, mains, edges, tables)


def solution(mesh):
    placed = (P("date", "space", None), P(), P(), P("date", None), P("date", None))
    return jax.shard_map(
        local, mesh=mesh, in_specs=placed, out_specs=P("date", None, "space", None), check_vma=False
    )
```

```python
import functools

import jax
import jax.numpy as jnp
import ml_dtypes
import numpy as np
from jax import lax
from jax.experimental import pallas as pl
from jax.experimental.layout import Layout, with_layout_constraint
from jax.experimental.pallas import tpu as pltpu
from jax.sharding import PartitionSpec as P

BF = jnp.bfloat16
F32 = jnp.float32
TILE = 16
SUB = 8


def constants(bins):
    k = np.arange(bins)
    angle = (k[:, None] * k[None, :] % bins) * (2.0 * np.pi / bins)
    cosine, sine = np.cos(angle), np.sin(angle)
    forward = np.block([[cosine, -sine], [sine, cosine]])
    inverse = np.block([[cosine, sine], [-sine, cosine]]) / bins
    half = bins // 2
    even, odd = np.arange(0, bins, 2), np.arange(1, bins, 2)
    even, odd = np.concatenate([even, bins + even]), np.concatenate([odd, bins + odd])
    first = np.concatenate([np.arange(half), bins + np.arange(half)])
    band = np.abs(k[:, None] - k[None, :]) <= 4
    made = (forward[:, np.concatenate([even, odd])], inverse[even][:, first], inverse[odd][:, first], band)
    return [jnp.asarray(m.astype(np.float32).astype(ml_dtypes.bfloat16)) for m in made]


def dot(a, b):
    return lax.dot_general(a, b, (((1,), (0,)), ((), ())), preferred_element_type=F32)


def pairs_kernel(block, count, partner, low, high, *refs, blocks):
    own, pool, edges, refs = refs[0], refs[1], refs[2 : 2 + blocks], refs[2 + blocks :]
    forward, inv_even, inv_odd, band, out = refs[:5]
    rims, sums, across, ready, out_sem = refs[5:]
    dates, slots = low.shape
    rows, cols = own.shape[1:]
    ext = rows + TILE
    bins = cols // 2
    half = bins // 2
    here = block[0]

    tile_row = lax.broadcasted_iota(jnp.int32, (TILE, cols), 0)
    for k in range(blocks):
        edge = dot(edges[k][...], forward[...]).astype(BF).astype(F32)
        for q in range(dates):
            before, after = edge[q : q + 1], edge[dates + q : dates + q + 1]
            tile = jnp.where(tile_row == 0, after, jnp.where(tile_row == TILE - 1, before, 0.0))
            rims[k * dates + q] = tile.astype(BF)

    lane = lax.broadcasted_iota(jnp.int32, (TILE, cols), 1)
    bin_id = lane % half * 2 + lane // bins
    even, odd, window = inv_even[...], inv_odd[...], band[...]

    def masked(date, slot):
        whole_date = here * dates + date
        live = slot < count[whole_date]
        low_bin = jnp.where(live, low[date, slot], 0)
        high_bin = jnp.where(live, high[date, slot], 0)
        mask = jnp.where((bin_id >= low_bin) & (bin_id < high_bin), 1.0, 0.0).astype(BF)[None]
        second = partner[whole_date, slot]
        away = second // dates - here
        away = jnp.where(away < 0, away + blocks, away)
        other = jnp.maximum(away - 1, 0) * dates + second % dates
        a = own[date].reshape(rows // TILE, TILE, cols) * mask
        b = pool[other].reshape(rows // TILE, TILE, cols) * mask
        a = jnp.concatenate([a.reshape(rows, cols), rims[date] * mask[0]], 0)
        b = jnp.concatenate([b.reshape(rows, cols), rims[dates + other] * mask[0]], 0)
        return [a, b]

    def filter_date(date, ring, group):
        x = jnp.concatenate([m for slot in group for m in masked(date, slot)], 0)
        e = dot(x[:, :bins], even)
        o = dot(x[:, bins:], odd)
        for i, slot in enumerate(group):
            r = slice(2 * i * ext, (2 * i + 2) * ext)
            for c, v in enumerate(((e[r] + o[r]).astype(BF), (e[r] - o[r]).astype(BF))):
                a_re, a_im, b_re, b_im = v[:ext, :half], v[:ext, half:], v[ext:, :half], v[ext:, half:]
                fields = (
                    a_re * b_re + a_im * b_im,
                    a_im * b_re - a_re * b_im,
                    a_re * a_re + a_im * a_im,
                    b_re * b_re + b_im * b_im,
                )
                for q, field in enumerate(fields):
                    sums[ring, slot, q * ext : (q + 1) * ext, c * half : (c + 1) * half] = field

    def look_date(ring, group, then=None):
        flat = jnp.concatenate([sums[ring, slot] for slot in group], 0)
        cut = flat.shape[0] // (2 * TILE) * TILE
        summed = jnp.concatenate([dot(flat[:cut], window), dot(flat[cut:], window)], 0)
        for i, slot in enumerate(group):
            looked = []
            for q in range(4):
                parts = []
                for c in range(2):
                    v = summed[(4 * i + q) * ext : (4 * i + q + 1) * ext, c * half : (c + 1) * half]
                    held = across.at[slot, 2 * q + c]
                    held[0:SUB] = v[ext - SUB :]
                    held[SUB:ext] = v[: ext - SUB]
                    up = pltpu.roll(v, 1, 0)[:rows] if q < 2 else held[SUB - 1 : SUB - 1 + rows]
                    parts.append(up + v[:rows] + held[SUB + 1 : SUB + 1 + rows])
                looked.append(jnp.concatenate(parts, 1))
            scale = lax.rsqrt(jnp.maximum(looked[2], 1.0) * jnp.maximum(looked[3], 1.0))
            ready[ring, slot, :, :bins] = (looked[0] * scale).astype(BF)
            ready[ring, slot, :, bins:] = (looked[1] * scale).astype(BF)
            if then is not None:
                then(slot)

    def send(date, ring):
        return pltpu.make_async_copy(ready.at[ring], out.at[date], out_sem.at[ring])

    parts_of_date = 1
    groups = [list(range(slots * g // parts_of_date, slots * (g + 1) // parts_of_date)) for g in range(parts_of_date)]
    groups = [g for g in groups if g]
    for group in groups:
        filter_date(0, 0, group)

    def body(date, _):
        now = lax.rem(date, 2)
        last = 1 - now

        @pl.when(date >= 3)
        def _():
            send(date - 3, last).wait()

        for group in groups:
            look_date(last, group)
            filter_date(date, now, group)
        send(date - 1, last).start()
        return 0

    lax.fori_loop(1, dates, body, 0)
    end = (dates - 1) % 2

    def send_slot(slot):
        pltpu.make_async_copy(ready.at[end, slot], out.at[dates - 1, slot], out_sem.at[end]).start()

    if dates >= 3:
        send(dates - 3, end).wait()
    for group in groups:
        look_date(end, group, send_slot)
    if dates >= 2:
        send(dates - 2, 1 - end).wait()
    send(dates - 1, end).wait()


def pairs(block, count, partner, low, high, mains, edges, tables):
    dates, rows, cols = mains[0].shape
    slots = partner.shape[1]
    ext = rows + TILE
    scalars = pl.BlockSpec(memory_space=pltpu.SMEM)
    whole = pl.BlockSpec(memory_space=pltpu.VMEM)
    anywhere = pl.BlockSpec(memory_space=pl.ANY)
    blocks = len(mains)
    pool = mains[1] if blocks == 2 else jnp.concatenate(mains[1:] or mains, 0)
    work = dates * slots * rows * cols
    return pl.pallas_call(
        functools.partial(pairs_kernel, blocks=blocks),
        in_specs=[scalars] * 5 + [whole] * (2 + blocks + len(tables)),
        out_specs=anywhere,
        out_shape=jax.ShapeDtypeStruct((dates, slots, rows, cols), BF),
        scratch_shapes=[
            pltpu.VMEM((blocks * dates, TILE, cols), BF),
            pltpu.VMEM((2, slots, 4 * ext, cols // 2), BF),
            pltpu.VMEM((slots, 8, ext, cols // 4), F32),
            pltpu.VMEM((2, slots, rows, cols), BF),
            pltpu.SemaphoreType.DMA((2,)),
        ],
        cost_estimate=pl.CostEstimate(flops=work * cols * 4, bytes_accessed=work * 2, transcendentals=work // 2),
        compiler_params=pltpu.CompilerParams(vmem_limit_bytes=50 * 2**20),
    )(block, count, partner, low, high, mains[0], pool, *edges, *tables)


def edge_rows(strips):
    n = lax.axis_size("space")
    even = lax.axis_index("space") % 2 == 0
    first, last = strips[:, 0, :], strips[:, -1, :]
    inner = [(i, i ^ 1) for i in range(n) if i ^ 1 < n]
    outer = [(i, i + 1) for i in range(1, n - 1, 2)] + [(i + 1, i) for i in range(1, n - 1, 2)]
    from_inner = lax.ppermute(jnp.where(even, last, first), "space", inner)
    from_outer = lax.ppermute(jnp.where(even, first, last), "space", outer)
    return jnp.concatenate([jnp.where(even, from_outer, from_inner), jnp.where(even, from_inner, from_outer)], 0)


def local(acquisitions, partner, pair_count, band_low, band_high):
    blocks = lax.axis_size("date")
    dates, rows, cols = acquisitions.shape
    tables = constants(cols // 2)

    def from_ahead(x, k):
        return lax.ppermute(x, "date", [((i + k) % blocks, i) for i in range(blocks)]) if k else x

    edge = edge_rows(acquisitions)
    mains = []
    for k in range(blocks):
        strip = from_ahead(acquisitions, k).reshape(dates * rows, cols)
        spectrum = jnp.dot(strip, tables[0], preferred_element_type=F32).astype(BF)
        spectrum = with_layout_constraint(spectrum, Layout(major_to_minor=(0, 1)))
        mains.append(spectrum.reshape(dates, rows, cols))
    edges = [from_ahead(edge, k) for k in range(blocks)]
    block = lax.axis_index("date").reshape(1).astype(jnp.int32)
    return pairs(block, pair_count, partner, band_low, band_high, mains, edges, tables)


def solution(mesh):
    placed = (P("date", "space", None), P(), P(), P("date", None), P("date", None))
    return jax.shard_map(
        local, mesh=mesh, in_specs=placed, out_specs=P("date", None, "space", None), check_vma=False
    )
```

```python
import functools

import jax
import jax.numpy as jnp
import ml_dtypes
import numpy as np
from jax import lax
from jax.experimental import pallas as pl
from jax.experimental.layout import Layout, with_layout_constraint
from jax.experimental.pallas import tpu as pltpu
from jax.sharding import PartitionSpec as P

BF = jnp.bfloat16
F32 = jnp.float32
TILE = 16
SUB = 8


def constants(bins):
    k = np.arange(bins)
    angle = (k[:, None] * k[None, :] % bins) * (2.0 * np.pi / bins)
    cosine, sine = np.cos(angle), np.sin(angle)
    forward = np.block([[cosine, -sine], [sine, cosine]])
    inverse = np.block([[cosine, sine], [-sine, cosine]]) / bins
    half = bins // 2
    even, odd = np.arange(0, bins, 2), np.arange(1, bins, 2)
    even, odd = np.concatenate([even, bins + even]), np.concatenate([odd, bins + odd])
    first = np.concatenate([np.arange(half), bins + np.arange(half)])
    band = np.abs(k[:, None] - k[None, :]) <= 4
    made = (forward[:, np.concatenate([even, odd])], inverse[even][:, first], inverse[odd][:, first], band)
    return [jnp.asarray(m.astype(np.float32).astype(ml_dtypes.bfloat16)) for m in made]


def dot(a, b):
    return lax.dot_general(a, b, (((1,), (0,)), ((), ())), preferred_element_type=F32)


def pairs_kernel(block, count, partner, low, high, *refs, blocks):
    own, pool, edges, refs = refs[0], refs[1], refs[2 : 2 + blocks], refs[2 + blocks :]
    forward, inv_even, inv_odd, band, out = refs[:5]
    rims, sums, across, ready, out_sem = refs[5:]
    dates, slots = low.shape
    rows, cols = own.shape[1:]
    ext = rows + TILE
    bins = cols // 2
    half = bins // 2
    here = block[0]

    tile_row = lax.broadcasted_iota(jnp.int32, (TILE, cols), 0)
    edge_spectra = dot(jnp.concatenate([edge[...] for edge in edges], 0), forward[...]).astype(BF).astype(F32)
    for k in range(blocks):
        edge = edge_spectra[2 * dates * k : 2 * dates * (k + 1)]
        for q in range(dates):
            before, after = edge[q : q + 1], edge[dates + q : dates + q + 1]
            tile = jnp.where(tile_row == 0, after, jnp.where(tile_row == TILE - 1, before, 0.0))
            rims[k * dates + q] = tile.astype(BF)

    lane = lax.broadcasted_iota(jnp.int32, (TILE, cols), 1)
    bin_id = lane % half * 2 + lane // bins
    even, odd, window = inv_even[...], inv_odd[...], band[...]

    def masked(date, slot):
        whole_date = here * dates + date
        live = slot < count[whole_date]
        low_bin = jnp.where(live, low[date, slot], 0)
        high_bin = jnp.where(live, high[date, slot], 0)
        mask = jnp.where((bin_id >= low_bin) & (bin_id < high_bin), 1.0, 0.0).astype(BF)[None]
        second = partner[whole_date, slot]
        away = second // dates - here
        away = jnp.where(away < 0, away + blocks, away)
        other = jnp.maximum(away - 1, 0) * dates + second % dates
        a = own[date].reshape(rows // TILE, TILE, cols) * mask
        b = pool[other].reshape(rows // TILE, TILE, cols) * mask
        a = jnp.concatenate([a.reshape(rows, cols), rims[date] * mask[0]], 0)
        b = jnp.concatenate([b.reshape(rows, cols), rims[dates + other] * mask[0]], 0)
        return [a, b]

    def filter_date(date, ring, group):
        x = jnp.concatenate([m for slot in group for m in masked(date, slot)], 0)
        e = dot(x[:, :bins], even)
        o = dot(x[:, bins:], odd)
        for i, slot in enumerate(group):
            r = slice(2 * i * ext, (2 * i + 2) * ext)
            for c, v in enumerate(((e[r] + o[r]).astype(BF), (e[r] - o[r]).astype(BF))):
                a_re, a_im, b_re, b_im = v[:ext, :half], v[:ext, half:], v[ext:, :half], v[ext:, half:]
                fields = (
                    a_re * b_re + a_im * b_im,
                    a_im * b_re - a_re * b_im,
                    a_re * a_re + a_im * a_im,
                    b_re * b_re + b_im * b_im,
                )
                for q, field in enumerate(fields):
                    sums[ring, slot, q * ext : (q + 1) * ext, c * half : (c + 1) * half] = field

    def look_date(ring, group, then=None):
        flat = jnp.concatenate([sums[ring, slot] for slot in group], 0)
        cut = flat.shape[0] // (2 * TILE) * TILE
        summed = jnp.concatenate([dot(flat[:cut], window), dot(flat[cut:], window)], 0)
        middle = (len(group) + 1) // 2
        turns = [i for pair in zip(range(middle), range(middle, len(group))) for i in pair]
        turns += list(range(len(group) // 2, middle))
        for i in turns:
            slot = group[i]
            looked = []
            for q in range(4):
                parts = []
                for c in range(2):
                    v = summed[(4 * i + q) * ext : (4 * i + q + 1) * ext, c * half : (c + 1) * half]
                    held = across.at[slot, 2 * q + c]
                    held[0:SUB] = v[ext - SUB :]
                    held[SUB:ext] = v[: ext - SUB]
                    up = pltpu.roll(v, 1, 0)[:rows] if q < 2 else held[SUB - 1 : SUB - 1 + rows]
                    parts.append(up + v[:rows] + held[SUB + 1 : SUB + 1 + rows])
                looked.append(jnp.concatenate(parts, 1))
            scale = lax.rsqrt(jnp.maximum(looked[2], 1.0) * jnp.maximum(looked[3], 1.0))
            ready[ring, slot, :, :bins] = (looked[0] * scale).astype(BF)
            ready[ring, slot, :, bins:] = (looked[1] * scale).astype(BF)
            if then is not None:
                then(slot)

    def send(date, ring):
        return pltpu.make_async_copy(ready.at[ring], out.at[date], out_sem.at[ring])

    parts_of_date = 1
    groups = [list(range(slots * g // parts_of_date, slots * (g + 1) // parts_of_date)) for g in range(parts_of_date)]
    groups = [g for g in groups if g]
    for group in groups:
        filter_date(0, 0, group)

    def body(date, _):
        now = lax.rem(date, 2)
        last = 1 - now

        @pl.when(date >= 3)
        def _():
            send(date - 3, last).wait()

        for group in groups:
            look_date(last, group)
            filter_date(date, now, group)
        send(date - 1, last).start()
        return 0

    lax.fori_loop(1, dates, body, 0)
    end = (dates - 1) % 2

    def send_slot(slot):
        pltpu.make_async_copy(ready.at[end, slot], out.at[dates - 1, slot], out_sem.at[end]).start()

    if dates >= 3:
        send(dates - 3, end).wait()
    for group in groups:
        look_date(end, group, send_slot)
    if dates >= 2:
        send(dates - 2, 1 - end).wait()
    send(dates - 1, end).wait()


def pairs(block, count, partner, low, high, mains, edges, tables):
    dates, rows, cols = mains[0].shape
    slots = partner.shape[1]
    ext = rows + TILE
    scalars = pl.BlockSpec(memory_space=pltpu.SMEM)
    whole = pl.BlockSpec(memory_space=pltpu.VMEM)
    anywhere = pl.BlockSpec(memory_space=pl.ANY)
    blocks = len(mains)
    pool = mains[1] if blocks == 2 else jnp.concatenate(mains[1:] or mains, 0)
    work = dates * slots * rows * cols
    return pl.pallas_call(
        functools.partial(pairs_kernel, blocks=blocks),
        in_specs=[scalars] * 5 + [whole] * (2 + blocks + len(tables)),
        out_specs=anywhere,
        out_shape=jax.ShapeDtypeStruct((dates, slots, rows, cols), BF),
        scratch_shapes=[
            pltpu.VMEM((blocks * dates, TILE, cols), BF),
            pltpu.VMEM((2, slots, 4 * ext, cols // 2), BF),
            pltpu.VMEM((slots, 8, ext, cols // 4), F32),
            pltpu.VMEM((2, slots, rows, cols), BF),
            pltpu.SemaphoreType.DMA((2,)),
        ],
        cost_estimate=pl.CostEstimate(flops=work * cols * 4, bytes_accessed=work * 2, transcendentals=work // 2),
        compiler_params=pltpu.CompilerParams(vmem_limit_bytes=50 * 2**20),
    )(block, count, partner, low, high, mains[0], pool, *edges, *tables)


def edge_rows(strips):
    n = lax.axis_size("space")
    even = lax.axis_index("space") % 2 == 0
    first, last = strips[:, 0, :], strips[:, -1, :]
    inner = [(i, i ^ 1) for i in range(n) if i ^ 1 < n]
    outer = [(i, i + 1) for i in range(1, n - 1, 2)] + [(i + 1, i) for i in range(1, n - 1, 2)]
    from_inner = lax.ppermute(jnp.where(even, last, first), "space", inner)
    from_outer = lax.ppermute(jnp.where(even, first, last), "space", outer)
    return jnp.concatenate([jnp.where(even, from_outer, from_inner), jnp.where(even, from_inner, from_outer)], 0)


def local(acquisitions, partner, pair_count, band_low, band_high):
    blocks = lax.axis_size("date")
    dates, rows, cols = acquisitions.shape
    tables = constants(cols // 2)

    def from_ahead(x, k):
        return lax.ppermute(x, "date", [((i + k) % blocks, i) for i in range(blocks)]) if k else x

    edge = edge_rows(acquisitions)
    mains = []
    for k in range(blocks):
        strip = from_ahead(acquisitions, k).reshape(dates * rows, cols)
        spectrum = jnp.dot(strip, tables[0], preferred_element_type=F32).astype(BF)
        spectrum = with_layout_constraint(spectrum, Layout(major_to_minor=(0, 1)))
        mains.append(spectrum.reshape(dates, rows, cols))
    edges = [from_ahead(edge, k) for k in range(blocks)]
    block = lax.axis_index("date").reshape(1).astype(jnp.int32)
    return pairs(block, pair_count, partner, band_low, band_high, mains, edges, tables)


def solution(mesh):
    placed = (P("date", "space", None), P(), P(), P("date", None), P("date", None))
    return jax.shard_map(
        local, mesh=mesh, in_specs=placed, out_specs=P("date", None, "space", None), check_vma=False
    )
```

```python
import functools

import jax
import jax.numpy as jnp
import ml_dtypes
import numpy as np
from jax import lax
from jax.experimental import pallas as pl
from jax.experimental.layout import Layout, with_layout_constraint
from jax.experimental.pallas import tpu as pltpu
from jax.sharding import PartitionSpec as P

BF = jnp.bfloat16
F32 = jnp.float32
TILE = 16
SUB = 8


def constants(bins):
    k = np.arange(bins)
    angle = (k[:, None] * k[None, :] % bins) * (2.0 * np.pi / bins)
    cosine, sine = np.cos(angle), np.sin(angle)
    forward = np.block([[cosine, -sine], [sine, cosine]])
    inverse = np.block([[cosine, sine], [-sine, cosine]]) / bins
    half = bins // 2
    even, odd = np.arange(0, bins, 2), np.arange(1, bins, 2)
    even, odd = np.concatenate([even, bins + even]), np.concatenate([odd, bins + odd])
    first = np.concatenate([np.arange(half), bins + np.arange(half)])
    band = np.abs(k[:, None] - k[None, :]) <= 4
    made = (forward[:, np.concatenate([even, odd])], inverse[even][:, first], inverse[odd][:, first], band)
    return [jnp.asarray(m.astype(np.float32).astype(ml_dtypes.bfloat16)) for m in made]


def dot(a, b):
    return lax.dot_general(a, b, (((1,), (0,)), ((), ())), preferred_element_type=F32)


def pairs_kernel(block, count, partner, low, high, *refs, blocks):
    own, pool, edges, refs = refs[0], refs[1], refs[2 : 2 + blocks], refs[2 + blocks :]
    forward, inv_even, inv_odd, band, out = refs[:5]
    rims, sums, across, ready, out_sem = refs[5:]
    dates, slots = low.shape
    rows, cols = own.shape[1:]
    ext = rows + TILE
    bins = cols // 2
    half = bins // 2
    here = block[0]

    tile_row = lax.broadcasted_iota(jnp.int32, (TILE, cols), 0)
    edge_spectra = dot(jnp.concatenate([edge[...] for edge in edges], 0), forward[...]).astype(BF).astype(F32)
    for k in range(blocks):
        edge = edge_spectra[2 * dates * k : 2 * dates * (k + 1)]
        for q in range(dates):
            before, after = edge[q : q + 1], edge[dates + q : dates + q + 1]
            tile = jnp.where(tile_row == 0, after, jnp.where(tile_row == TILE - 1, before, 0.0))
            rims[k * dates + q] = tile.astype(BF)

    lane = lax.broadcasted_iota(jnp.int32, (TILE, cols), 1)
    bin_id = lane % half * 2 + lane // bins
    even, odd, window = inv_even[...], inv_odd[...], band[...]

    def masked(date, slot):
        whole_date = here * dates + date
        live = slot < count[whole_date]
        low_bin = jnp.where(live, low[date, slot], 0)
        high_bin = jnp.where(live, high[date, slot], 0)
        mask = jnp.where((bin_id >= low_bin) & (bin_id < high_bin), 1.0, 0.0).astype(BF)[None]
        second = partner[whole_date, slot]
        away = second // dates - here
        away = jnp.where(away < 0, away + blocks, away)
        other = jnp.maximum(away - 1, 0) * dates + second % dates
        a = own[date].reshape(rows // TILE, TILE, cols) * mask
        b = pool[other].reshape(rows // TILE, TILE, cols) * mask
        a = jnp.concatenate([a.reshape(rows, cols), rims[date] * mask[0]], 0)
        b = jnp.concatenate([b.reshape(rows, cols), rims[dates + other] * mask[0]], 0)
        return [a, b]

    def filter_date(date, ring, group):
        x = jnp.concatenate([m for slot in group for m in masked(date, slot)], 0)
        e = dot(x[:, :bins], even)
        o = dot(x[:, bins:], odd)
        for i, slot in enumerate(group):
            r = slice(2 * i * ext, (2 * i + 2) * ext)
            for c, v in enumerate(((e[r] + o[r]).astype(BF), (e[r] - o[r]).astype(BF))):
                a_re, a_im, b_re, b_im = v[:ext, :half], v[:ext, half:], v[ext:, :half], v[ext:, half:]
                fields = (
                    a_re * b_re + a_im * b_im,
                    a_im * b_re - a_re * b_im,
                    a_re * a_re + a_im * a_im,
                    b_re * b_re + b_im * b_im,
                )
                for q, field in enumerate(fields):
                    sums[ring, slot, q * ext : (q + 1) * ext, c * half : (c + 1) * half] = field

    def look_date(ring, group, then=None):
        flat = jnp.concatenate([sums[ring, slot] for slot in group], 0)
        cut = flat.shape[0] // (2 * TILE) * TILE
        summed = jnp.concatenate([dot(flat[:cut], window), dot(flat[cut:], window)], 0)
        middle = (len(group) + 1) // 2
        turns = [i for pair in zip(range(middle), range(middle, len(group))) for i in pair]
        turns += list(range(len(group) // 2, middle))
        for i in turns:
            slot = group[i]
            looked = []
            for q in range(4):
                parts = []
                for c in range(2):
                    v = summed[(4 * i + q) * ext : (4 * i + q + 1) * ext, c * half : (c + 1) * half]
                    held = across.at[slot, 2 * q + c]
                    held[0:SUB] = v[ext - SUB :]
                    held[SUB:ext] = v[: ext - SUB]
                    up = pltpu.roll(v, 1, 0)[:rows] if q >= 2 else held[SUB - 1 : SUB - 1 + rows]
                    parts.append(up + v[:rows] + held[SUB + 1 : SUB + 1 + rows])
                looked.append(jnp.concatenate(parts, 1))
            scale = lax.rsqrt(jnp.maximum(looked[2], 1.0) * jnp.maximum(looked[3], 1.0))
            ready[ring, slot, :, :bins] = (looked[0] * scale).astype(BF)
            ready[ring, slot, :, bins:] = (looked[1] * scale).astype(BF)
            if then is not None:
                then(slot)

    def send(date, ring):
        return pltpu.make_async_copy(ready.at[ring], out.at[date], out_sem.at[ring])

    parts_of_date = 1
    groups = [list(range(slots * g // parts_of_date, slots * (g + 1) // parts_of_date)) for g in range(parts_of_date)]
    groups = [g for g in groups if g]
    for group in groups:
        filter_date(0, 0, group)

    def body(date, _):
        now = lax.rem(date, 2)
        last = 1 - now

        @pl.when(date >= 3)
        def _():
            send(date - 3, last).wait()

        for group in groups:
            look_date(last, group)
            filter_date(date, now, group)
        send(date - 1, last).start()
        return 0

    lax.fori_loop(1, dates, body, 0)
    end = (dates - 1) % 2

    def send_slot(slot):
        pltpu.make_async_copy(ready.at[end, slot], out.at[dates - 1, slot], out_sem.at[end]).start()

    if dates >= 3:
        send(dates - 3, end).wait()
    for group in groups:
        look_date(end, group, send_slot)
    if dates >= 2:
        send(dates - 2, 1 - end).wait()
    send(dates - 1, end).wait()


def pairs(block, count, partner, low, high, mains, edges, tables):
    dates, rows, cols = mains[0].shape
    slots = partner.shape[1]
    ext = rows + TILE
    scalars = pl.BlockSpec(memory_space=pltpu.SMEM)
    whole = pl.BlockSpec(memory_space=pltpu.VMEM)
    anywhere = pl.BlockSpec(memory_space=pl.ANY)
    blocks = len(mains)
    pool = mains[1] if blocks == 2 else jnp.concatenate(mains[1:] or mains, 0)
    work = dates * slots * rows * cols
    return pl.pallas_call(
        functools.partial(pairs_kernel, blocks=blocks),
        in_specs=[scalars] * 5 + [whole] * (2 + blocks + len(tables)),
        out_specs=anywhere,
        out_shape=jax.ShapeDtypeStruct((dates, slots, rows, cols), BF),
        scratch_shapes=[
            pltpu.VMEM((blocks * dates, TILE, cols), BF),
            pltpu.VMEM((2, slots, 4 * ext, cols // 2), BF),
            pltpu.VMEM((slots, 8, ext, cols // 4), F32),
            pltpu.VMEM((2, slots, rows, cols), BF),
            pltpu.SemaphoreType.DMA((2,)),
        ],
        cost_estimate=pl.CostEstimate(flops=work * cols * 4, bytes_accessed=work * 2, transcendentals=work // 2),
        compiler_params=pltpu.CompilerParams(vmem_limit_bytes=50 * 2**20),
    )(block, count, partner, low, high, mains[0], pool, *edges, *tables)


def edge_rows(strips):
    n = lax.axis_size("space")
    even = lax.axis_index("space") % 2 == 0
    first, last = strips[:, 0, :], strips[:, -1, :]
    inner = [(i, i ^ 1) for i in range(n) if i ^ 1 < n]
    outer = [(i, i + 1) for i in range(1, n - 1, 2)] + [(i + 1, i) for i in range(1, n - 1, 2)]
    from_inner = lax.ppermute(jnp.where(even, last, first), "space", inner)
    from_outer = lax.ppermute(jnp.where(even, first, last), "space", outer)
    return jnp.concatenate([jnp.where(even, from_outer, from_inner), jnp.where(even, from_inner, from_outer)], 0)


def local(acquisitions, partner, pair_count, band_low, band_high):
    blocks = lax.axis_size("date")
    dates, rows, cols = acquisitions.shape
    tables = constants(cols // 2)

    def from_ahead(x, k):
        return lax.ppermute(x, "date", [((i + k) % blocks, i) for i in range(blocks)]) if k else x

    edge = edge_rows(acquisitions)
    mains = []
    for k in range(blocks):
        strip = from_ahead(acquisitions, k).reshape(dates * rows, cols)
        spectrum = jnp.dot(strip, tables[0], preferred_element_type=F32).astype(BF)
        spectrum = with_layout_constraint(spectrum, Layout(major_to_minor=(0, 1)))
        mains.append(spectrum.reshape(dates, rows, cols))
    edges = [from_ahead(edge, k) for k in range(blocks)]
    block = lax.axis_index("date").reshape(1).astype(jnp.int32)
    return pairs(block, pair_count, partner, band_low, band_high, mains, edges, tables)


def solution(mesh):
    placed = (P("date", "space", None), P(), P(), P("date", None), P("date", None))
    return jax.shard_map(
        local, mesh=mesh, in_specs=placed, out_specs=P("date", None, "space", None), check_vma=False
    )
```
